32 devices in a mesh: grp: 2 (over y), ex: 4 (over z), lay: 4 (over x, core).
Axes of the slice: x: 2, y: 2, z: 4, core: 2. Of those that a mesh axis runs over, the one named last changes fastest.
Arguments:
- train_grads: bfloat16 [4, 16384, 1024], P('lay', ('grp', 'ex')), parts along dimension 1, may hold values from -0.796875 to 0.796875
- queries: bfloat16 [4, 512, 1024], P('lay', ('grp', 'ex')), parts along dimension 1, may hold values from -0.23925781 to 0.23925781
- out_basis: float32 [4, 32, 32], P('lay'), may hold values from -1 to 1
- in_basis: float32 [4, 32, 32], P('lay'), may hold values from -1 to 1
- eigenvalues: float32 [4, 32, 32], P('lay'), may hold values from 0.05 to 5
Outputs:
- scores: bfloat16 [512, 8192], P('grp', ('ex', 'lay')), parts along dimension 0
The draws below stay inside these ranges and needn't reach their ends.
There are 2 independent parts, one for each index of `grp`. The reference program is written for one: setup_inputs(seed, part) draws one part's arguments, and reference() takes and returns one part's arrays. A program takes and returns all parts, laid end to end along the dimension named above; an argument that names none is the same for every part. Nothing has to cross between parts.
All inputs are finite; a program needn't handle non-finite values.
Results may differ from the reference program's by a relative error of at most 0.0095.
Values may be sent and summed in bfloat16 or wider, within the bound.
A program may use at most 64 MiB of HBM per device.

```python
import math
import jax
import jax.numpy as jnp
from jax import lax

R_OUT = 32
R_IN = 32
LAY_DEV = 1
FLAT = 1024
LAYERS = 4
NT = 8192
NQ = 256
N_LAY = 4


def shard_levels(own_key, dims, split, low, top_value):
    def one(axis_at, shards_of):
        heights = jax.random.uniform(jax.random.fold_in(jax.random.fold_in(own_key, 6), axis_at), (shards_of,), jnp.float32, low / len(split), top_value / len(split))
        return jnp.repeat(jnp.exp(heights), dims[axis_at] // shards_of).reshape((-1,) + (1,) * (len(dims) - axis_at - 1))

    loudness = one(*split[0])
    for cut in split[1:]:
        loudness = loudness * one(*cut)
    return loudness


def normal_values(key, dims, deviation, most, split=(), held_as=jnp.bfloat16):
    loudness = shard_levels(key, dims, split, -0.22, 0.18) if split else 1.0
    entries = jax.random.normal(key, dims, jnp.float32) * deviation * loudness
    return jnp.minimum(jnp.maximum(entries, -most), most).astype(held_as)


def setup_inputs(seed: int = 0, part: int = 0) -> dict:
    keys = jax.random.split(jax.random.key(seed), 6)
    part_splits = jax.random.split(jax.random.fold_in(keys[5], part), 6)
    train_grads = normal_values(part_splits[0], (LAYERS, NT, FLAT), 0.1, 0.796875, ((0, 4), (1, 4)))
    queries = normal_values(part_splits[1], (LAYERS, NQ, FLAT), 0.03, 0.23925781, ((0, 4), (1, 4)))
    out_basis = normal_values(keys[2], (LAYERS, R_OUT, R_OUT), R_OUT ** -0.5, 1.0, ((0, 4),), jnp.float32)
    in_basis = normal_values(keys[3], (LAYERS, R_IN, R_IN), R_IN ** -0.5, 1.0, ((0, 4),), jnp.float32)
    eigenvalues = jnp.clip(jnp.exp(math.log(5.0) - 4.6051702 * jax.random.uniform(keys[4], (LAYERS, R_OUT, R_IN), jnp.float32) ** shard_levels(keys[4], (LAYERS, R_OUT, R_IN), ((0, 4),), -0.2, 0.2)), 0.05, 5.0)
    return {"train_grads": train_grads, "queries": queries, "out_basis": out_basis, "in_basis": in_basis, "eigenvalues": eigenvalues}


def condition(grads, out_mat, in_mat, eigen):
    count = grads.shape[0]
    square = grads.astype(jnp.float32).reshape(count, out_mat.shape[0], in_mat.shape[0])
    rotated = jnp.einsum("aj,nab,bk->njk", out_mat, square, in_mat, precision=lax.Precision.HIGHEST)
    damping = 0.1 * jnp.mean(eigen)
    damped = rotated / (eigen + damping)
    restored = jnp.einsum("aj,njk,bk->nab", out_mat, damped, in_mat, precision=lax.Precision.HIGHEST)
    return restored.reshape(count, out_mat.shape[0] * in_mat.shape[0]).astype(jnp.bfloat16)


def reference(train_grads, queries, out_basis, in_basis, eigenvalues):
    def group(total, index):
        partial_sum = jnp.zeros((queries.shape[1], train_grads.shape[1]), jnp.float32)
        for inner in range(LAY_DEV):
            layer = (index * LAY_DEV + inner).astype(jnp.int32)
            grads = lax.dynamic_index_in_dim(train_grads, layer, 0, keepdims=False)
            query_rows = lax.dynamic_index_in_dim(queries, layer, 0, keepdims=False)
            out_mat = lax.dynamic_index_in_dim(out_basis, layer, 0, keepdims=False)
            in_mat = lax.dynamic_index_in_dim(in_basis, layer, 0, keepdims=False)
            eigen = lax.dynamic_index_in_dim(eigenvalues, layer, 0, keepdims=False)
            conditioned = condition(query_rows, out_mat, in_mat, eigen)
            partial_sum = partial_sum + jnp.dot(conditioned, grads.T, preferred_element_type=jnp.float32)
        rounded = lax.optimization_barrier(partial_sum.astype(jnp.bfloat16))
        return total + rounded.astype(jnp.float32), None

    start = jnp.zeros((queries.shape[1], train_grads.shape[1]), jnp.float32)
    total, _ = lax.scan(group, start, jnp.arange(N_LAY, dtype=jnp.int32))
    return total.astype(jnp.bfloat16)
```

```python
import functools

import jax
import jax.numpy as jnp
from jax import lax
from jax.experimental import pallas as pl
from jax.experimental.pallas import tpu as pltpu
from jax.sharding import PartitionSpec as P

MESH = pl.DeviceIdType.MESH
F32 = jnp.float32
BF16 = jnp.bfloat16
PIECES = 2


def dot(a, b):
    return lax.dot_general(a, b, (((1,), (0,)), ((), ())), preferred_element_type=F32)


def dot_t(a, b):
    return lax.dot_general(a, b, (((1,), (1,)), ((), ())), preferred_element_type=F32)


def exact_dot(a, b):
    return jnp.dot(a, b, precision=lax.Precision.HIGHEST, preferred_element_type=F32)


def split(value):
    high = value.astype(BF16)
    return high, (value - high.astype(F32)).astype(BF16)


def kernel(
    n_ex, n_x,
    train_ref, query_ref, out_basis_ref, in_basis_ref, eigen_ref, scores_ref,
    train, held, out_mat, in_mat, eigen, wide_out, high, low, inverse,
    to_core, from_core, keep, to_chip, from_chip,
    local_sem, train_sem, gather_send, gather_recv, core_send, core_recv, chip_send, chip_recv,
):
    ex = lax.axis_index("ex")
    lay = lax.axis_index("lay")
    core = lax.rem(lay, 2)
    x = lax.div(lay, 2)
    n_lay = 2 * n_x
    width = train.shape[0] // n_lay
    count, flat = held.shape[1], held.shape[2]
    r_out, r_in = out_mat.shape[0], in_mat.shape[0]
    piece = count // PIECES
    middle = jnp.logical_and(ex > 0, ex < n_ex - 1)

    small = [
        pltpu.make_async_copy(out_basis_ref.at[0], out_mat, local_sem.at[0]),
        pltpu.make_async_copy(in_basis_ref.at[0], in_mat, local_sem.at[1]),
        pltpu.make_async_copy(eigen_ref.at[0], eigen, local_sem.at[2]),
        pltpu.make_async_copy(query_ref.at[0], held.at[ex], local_sem.at[3]),
    ]
    for copy in small:
        copy.start()

    barrier = pltpu.get_barrier_semaphore()

    @pl.when(ex > 0)
    def _():
        pl.semaphore_signal(barrier, inc=1, device_id={"ex": ex - 1}, device_id_type=MESH)

    @pl.when(ex < n_ex - 1)
    def _():
        pl.semaphore_signal(barrier, inc=1, device_id={"ex": ex + 1}, device_id_type=MESH)

    sibling = 2 * x + 1 - core
    pl.semaphore_signal(barrier, inc=1, device_id={"lay": sibling}, device_id_type=MESH)
    for step in range(1, n_x):
        other = lax.rem(x + step, n_x)
        pl.semaphore_signal(barrier, inc=1, device_id={"lay": 2 * other + core}, device_id_type=MESH)

    @pl.when(middle)
    def _():
        pl.semaphore_wait(barrier, n_x + 2)

    @pl.when(jnp.logical_not(middle))
    def _():
        pl.semaphore_wait(barrier, n_x + 1)

    def passing(shard, part, way, own=False):
        rows = pl.ds(part * piece, piece)
        return pltpu.make_async_remote_copy(
            src_ref=query_ref.at[0, rows] if own else held.at[shard, rows],
            dst_ref=held.at[shard, rows],
            send_sem=gather_send.at[way, shard, part],
            recv_sem=gather_recv.at[shard, part],
            device_id={"ex": ex + 2 * way - 1},
            device_id_type=MESH,
        )

    for part in range(PIECES):
        @pl.when(ex > 0)
        def _():
            passing(ex, part, 0, True).start()

        @pl.when(ex < n_ex - 1)
        def _():
            passing(ex, part, 1, True).start()

    blocks = [
        pltpu.make_async_copy(
            train_ref.at[0, pl.ds(g * width, width)], train.at[pl.ds(g * width, width)], train_sem.at[g]
        )
        for g in range(n_lay)
    ]
    for copy in blocks:
        copy.start()

    both = jnp.minimum(ex, n_ex - 1 - ex)

    def shard_of(step):
        near = lax.div(step + 1, 2)
        near_shard = jnp.where(lax.rem(step, 2) == 1, ex - near, ex + near)
        far = step - both
        far_shard = jnp.where(2 * ex < n_ex - 1, ex + far, ex - far)
        return jnp.where(step <= 2 * both, near_shard, far_shard)

    def arrive(step):
        shard = shard_of(step)
        for part in range(PIECES):
            passing(shard, part, 0).wait_recv()

            @pl.when(jnp.logical_and(shard > ex, ex > 0))
            def _():
                passing(shard, part, 0).start()

            @pl.when(jnp.logical_and(shard < ex, ex < n_ex - 1))
            def _():
                passing(shard, part, 1).start()

    for copy in small:
        copy.wait()
    column = lax.broadcasted_iota(jnp.int32, (r_in, flat), 1)
    inner = (lax.rem(column, r_in) == lax.broadcasted_iota(jnp.int32, (r_in, flat), 0)).astype(F32)
    outer_mask = lax.div(
        lax.broadcasted_iota(jnp.int32, (r_out, flat), 1), r_in
    ) == lax.broadcasted_iota(jnp.int32, (r_out, flat), 0)
    wide_out[...] = exact_dot(out_mat[...], outer_mask.astype(F32))
    wide_in = exact_dot(in_mat[...], inner)
    wide_eigen = exact_dot(eigen[...], inner)
    damping = 0.1 * jnp.mean(eigen[...])
    line = jnp.sum(jnp.where(outer_mask, wide_eigen, 0.0), axis=0, keepdims=True)
    inverse[...] = 1.0 / (line + damping)

    for a in range(r_out):
        above, below = split(wide_in * wide_out[a : a + 1, :])
        high[a * r_in : (a + 1) * r_in, :] = above
        low[a * r_in : (a + 1) * r_in, :] = below

    @pl.when(middle)
    def _():
        arrive(1)
        arrive(2)

    for copy in blocks:
        copy.wait()

    def core_copy(step):
        return pltpu.make_async_remote_copy(
            src_ref=to_core.at[step],
            dst_ref=from_core.at[step],
            send_sem=core_send.at[step],
            recv_sem=core_recv.at[step],
            device_id={"lay": sibling},
            device_id_type=MESH,
        )

    def chip_copy(step, other):
        return pltpu.make_async_remote_copy(
            src_ref=to_chip.at[step, other],
            dst_ref=from_chip.at[step, x],
            send_sem=chip_send.at[step, other],
            recv_sem=chip_recv.at[step, x],
            device_id={"lay": 2 * other + core},
            device_id_type=MESH,
        )

    def chip_arrival(step, other):
        return pltpu.make_async_remote_copy(
            src_ref=to_chip.at[step, other],
            dst_ref=from_chip.at[step, other],
            send_sem=chip_send.at[step, other],
            recv_sem=chip_recv.at[step, other],
            device_id={"lay": 2 * other + core},
            device_id_type=MESH,
        )

    def score(step):
        shard = shard_of(step)
        query = held[shard]
        rotated = dot(query, high[...]) + dot(query, low[...])
        above, below = split(rotated * inverse[...])
        conditioned = (
            dot_t(above, high[...]) + dot_t(below, high[...]) + dot_t(above, low[...])
        ).astype(BF16)
        for other in range(n_x):
            rows = pl.ds(pl.multiple_of((2 * other + 1 - core) * width, width), width)
            to_core[step, other] = dot_t(conditioned, train[rows, :]).astype(BF16)
        core_copy(step).start()
        for other in range(n_x):
            rows = pl.ds(pl.multiple_of((2 * other + core) * width, width), width)
            keep[step, other] = dot_t(conditioned, train[rows, :])

    def pair(step):
        core_copy(step).wait_recv()
        for hop in range(1, n_x):
            other = lax.rem(x + hop, n_x)
            to_chip[step, other] = (keep[step, other] + from_core[step, other].astype(F32)).astype(BF16)
            chip_copy(step, other).start()

    def finish(step):
        total = keep[step, x] + from_core[step, x].astype(F32)
        for hop in range(1, n_x):
            other = lax.rem(x + hop, n_x)
            chip_arrival(step, other).wait_recv()
            total += from_chip[step, other].astype(F32)
        rows = pl.ds(pl.multiple_of(shard_of(step) * count, count), count)
        scores_ref[rows, :] = total.astype(BF16)

    def turn(step, carry):
        @pl.when(jnp.logical_and(jnp.logical_not(middle), step >= 1))
        def _():
            arrive(step)

        @pl.when(jnp.logical_and(middle, jnp.logical_and(step >= 2, step < n_ex - 1)))
        def _():
            arrive(step + 1)

        score(step)

        @pl.when(step >= 1)
        def _():
            pair(step - 1)

        @pl.when(step >= 2)
        def _():
            finish(step - 2)

        return carry

    lax.fori_loop(0, n_ex, turn, 0)
    pair(n_ex - 1)
    if n_ex > 1:
        finish(n_ex - 2)
    finish(n_ex - 1)

    for part in range(PIECES):
        @pl.when(ex > 0)
        def _():
            passing(ex, part, 0, True).wait_send()

        @pl.when(ex < n_ex - 1)
        def _():
            passing(ex, part, 1, True).wait_send()

    def drain(step, carry):
        core_copy(step).wait_send()
        for hop in range(1, n_x):
            chip_copy(step, lax.rem(x + hop, n_x)).wait_send()

        @pl.when(step >= 1)
        def _():
            shard = shard_of(step)
            for part in range(PIECES):
                @pl.when(jnp.logical_and(shard > ex, ex > 0))
                def _():
                    passing(shard, part, 0).wait_send()

                @pl.when(jnp.logical_and(shard < ex, ex < n_ex - 1))
                def _():
                    passing(shard, part, 1).wait_send()

        return carry

    lax.fori_loop(0, n_ex, drain, 0)


def on_device(n_ex, n_lay, train_grads, queries, out_basis, in_basis, eigenvalues):
    n_x = n_lay // 2
    trains, flat = train_grads.shape[1:]
    count = queries.shape[1]
    width = trains // n_lay
    r_out, r_in = out_basis.shape[1], in_basis.shape[1]
    anywhere = pl.BlockSpec(memory_space=pl.ANY)
    dma = pltpu.SemaphoreType.DMA
    return pl.pallas_call(
        functools.partial(kernel, n_ex, n_x),
        out_shape=jax.ShapeDtypeStruct((n_ex * count, width), BF16),
        in_specs=[anywhere] * 5,
        out_specs=pl.BlockSpec(memory_space=pltpu.VMEM),
        scratch_shapes=[
            pltpu.VMEM((trains, flat), BF16),
            pltpu.VMEM((n_ex, count, flat), BF16),
            pltpu.VMEM((r_out, r_out), F32),
            pltpu.VMEM((r_in, r_in), F32),
            pltpu.VMEM((r_out, r_in), F32),
            pltpu.VMEM((r_out, flat), F32),
            pltpu.VMEM((flat, flat), BF16),
            pltpu.VMEM((flat, flat), BF16),
            pltpu.VMEM((1, flat), F32),
            pltpu.VMEM((n_ex, n_x, count, width), BF16),
            pltpu.VMEM((n_ex, n_x, count, width), BF16),
            pltpu.VMEM((n_ex, n_x, count, width), F32),
            pltpu.VMEM((n_ex, n_x, count, width), BF16),
            pltpu.VMEM((n_ex, n_x, count, width), BF16),
            dma((4,)),
            dma((n_lay,)),
            dma((2, n_ex, PIECES)),
            dma((n_ex, PIECES)),
            dma((n_ex,)),
            dma((n_ex,)),
            dma((n_ex, n_x)),
            dma((n_ex, n_x)),
        ],
        compiler_params=pltpu.CompilerParams(
            collective_id=0, has_side_effects=True, vmem_limit_bytes=56 * 1024 * 1024
        ),
        cost_estimate=pl.CostEstimate(
            flops=2 * n_ex * count * flat * (trains + 5 * flat),
            bytes_accessed=2 * (trains + count) * flat,
            transcendentals=0,
        ),
    )(train_grads, queries, out_basis, in_basis, eigenvalues)


def solution(mesh):
    placed = (
        P("lay", ("grp", "ex"), None),
        P("lay", ("grp", "ex"), None),
        P("lay", None, None),
        P("lay", None, None),
        P("lay", None, None),
    )
    return jax.shard_map(
        functools.partial(on_device, mesh.shape["ex"], mesh.shape["lay"]),
        mesh=mesh,
        in_specs=placed,
        out_specs=P("grp", ("ex", "lay")),
        check_vma=False,
    )
```

```python
import functools

import jax
import jax.numpy as jnp
from jax import lax
from jax.experimental import pallas as pl
from jax.experimental.pallas import tpu as pltpu
from jax.sharding import PartitionSpec as P

MESH = pl.DeviceIdType.MESH
F32 = jnp.float32
BF16 = jnp.bfloat16
PIECES = 2


def dot(a, b):
    return lax.dot_general(a, b, (((1,), (0,)), ((), ())), preferred_element_type=F32)


def exact_dot(a, b):
    return jnp.dot(a, b, precision=lax.Precision.HIGHEST, preferred_element_type=F32)


def split(value):
    high = value.astype(BF16)
    return high, (value - high.astype(F32)).astype(BF16)


def kernel(
    n_ex, n_x,
    train_ref, query_ref, out_basis_ref, in_basis_ref, eigen_ref, scores_ref,
    train, train_t, held, out_mat, in_mat, eigen, wide_out, high, low, high_t, low_t, inverse,
    to_core, from_core, keep, to_chip, from_chip,
    local_sem, train_sem, gather_send, gather_recv, core_send, core_recv, chip_send, chip_recv,
):
    ex = lax.axis_index("ex")
    lay = lax.axis_index("lay")
    core = lax.rem(lay, 2)
    x = lax.div(lay, 2)
    n_lay = 2 * n_x
    width = train.shape[0] // n_lay
    count, flat = held.shape[1], held.shape[2]
    r_out, r_in = out_mat.shape[0], in_mat.shape[0]
    piece = count // PIECES
    middle = jnp.logical_and(ex > 0, ex < n_ex - 1)

    small = [
        pltpu.make_async_copy(out_basis_ref.at[0], out_mat, local_sem.at[0]),
        pltpu.make_async_copy(in_basis_ref.at[0], in_mat, local_sem.at[1]),
        pltpu.make_async_copy(eigen_ref.at[0], eigen, local_sem.at[2]),
        pltpu.make_async_copy(query_ref.at[0], held.at[ex], local_sem.at[3]),
    ]
    for copy in small:
        copy.start()

    barrier = pltpu.get_barrier_semaphore()

    @pl.when(ex > 0)
    def _():
        pl.semaphore_signal(barrier, inc=1, device_id={"ex": ex - 1}, device_id_type=MESH)

    @pl.when(ex < n_ex - 1)
    def _():
        pl.semaphore_signal(barrier, inc=1, device_id={"ex": ex + 1}, device_id_type=MESH)

    sibling = 2 * x + 1 - core
    pl.semaphore_signal(barrier, inc=1, device_id={"lay": sibling}, device_id_type=MESH)
    for step in range(1, n_x):
        other = lax.rem(x + step, n_x)
        pl.semaphore_signal(barrier, inc=1, device_id={"lay": 2 * other + core}, device_id_type=MESH)

    @pl.when(middle)
    def _():
        pl.semaphore_wait(barrier, n_x + 2)

    @pl.when(jnp.logical_not(middle))
    def _():
        pl.semaphore_wait(barrier, n_x + 1)

    def passing(shard, part, way, own=False):
        rows = pl.ds(part * piece, piece)
        return pltpu.make_async_remote_copy(
            src_ref=query_ref.at[0, rows] if own else held.at[shard, rows],
            dst_ref=held.at[shard, rows],
            send_sem=gather_send.at[way, shard, part],
            recv_sem=gather_recv.at[shard, part],
            device_id={"ex": ex + 2 * way - 1},
            device_id_type=MESH,
        )

    for part in range(PIECES):
        @pl.when(ex > 0)
        def _():
            passing(ex, part, 0, True).start()

        @pl.when(ex < n_ex - 1)
        def _():
            passing(ex, part, 1, True).start()

    blocks = [
        pltpu.make_async_copy(
            train_ref.at[0, pl.ds(g * width, width)], train.at[pl.ds(g * width, width)], train_sem.at[g]
        )
        for g in range(n_lay)
    ]
    for copy in blocks:
        copy.start()

    both = jnp.minimum(ex, n_ex - 1 - ex)

    def shard_of(step):
        near = lax.div(step + 1, 2)
        near_shard = jnp.where(lax.rem(step, 2) == 1, ex - near, ex + near)
        far = step - both
        far_shard = jnp.where(2 * ex < n_ex - 1, ex + far, ex - far)
        return jnp.where(step <= 2 * both, near_shard, far_shard)

    def arrive(step):
        shard = shard_of(step)
        for part in range(PIECES):
            passing(shard, part, 0).wait_recv()

            @pl.when(jnp.logical_and(shard > ex, ex > 0))
            def _():
                passing(shard, part, 0).start()

            @pl.when(jnp.logical_and(shard < ex, ex < n_ex - 1))
            def _():
                passing(shard, part, 1).start()

    for copy in small:
        copy.wait()
    column = lax.broadcasted_iota(jnp.int32, (r_in, flat), 1)
    inner = (lax.rem(column, r_in) == lax.broadcasted_iota(jnp.int32, (r_in, flat), 0)).astype(F32)
    outer_mask = lax.div(
        lax.broadcasted_iota(jnp.int32, (r_out, flat), 1), r_in
    ) == lax.broadcasted_iota(jnp.int32, (r_out, flat), 0)
    outer = outer_mask.astype(F32)
    wide_eigen = exact_dot(eigen[...], inner)
    damping = 0.1 * jnp.mean(eigen[...])
    line = jnp.sum(jnp.where(outer_mask, wide_eigen, 0.0), axis=0, keepdims=True)
    inverse[...] = 1.0 / (line + damping)

    def spread(out_part, in_part, above_ref, below_ref):
        wide_out[...] = exact_dot(out_part, outer)
        wide_in = exact_dot(in_part, inner)
        for a in range(r_out):
            above, below = split(wide_in * wide_out[a : a + 1, :])
            above_ref[a * r_in : (a + 1) * r_in, :] = above
            below_ref[a * r_in : (a + 1) * r_in, :] = below

    spread(out_mat[...], in_mat[...], high, low)
    spread(out_mat[...].T, in_mat[...].T, high_t, low_t)

    @pl.when(middle)
    def _():
        arrive(1)
        arrive(2)

    for g, copy in enumerate(blocks):
        copy.wait()
        span = slice(g * width, (g + 1) * width)
        train_t[:, span] = train[span, :].T

    @pl.when(jnp.logical_not(middle))
    def _():
        arrive(1)

    def core_copy(step):
        return pltpu.make_async_remote_copy(
            src_ref=to_core.at[step],
            dst_ref=from_core.at[step],
            send_sem=core_send.at[step],
            recv_sem=core_recv.at[step],
            device_id={"lay": sibling},
            device_id_type=MESH,
        )

    def chip_copy(step, other):
        return pltpu.make_async_remote_copy(
            src_ref=to_chip.at[step, other],
            dst_ref=from_chip.at[step, x],
            send_sem=chip_send.at[step, other],
            recv_sem=chip_recv.at[step, x],
            device_id={"lay": 2 * other + core},
            device_id_type=MESH,
        )

    def chip_arrival(step, other):
        return pltpu.make_async_remote_copy(
            src_ref=to_chip.at[step, other],
            dst_ref=from_chip.at[step, other],
            send_sem=chip_send.at[step, other],
            recv_sem=chip_recv.at[step, other],
            device_id={"lay": 2 * other + core},
            device_id_type=MESH,
        )

    def score(steps):
        query = jnp.concatenate([held[shard_of(step)] for step in steps], axis=0)
        rotated = dot(query, high[...]) + dot(query, low[...])
        above, below = split(rotated * inverse[...])
        stacked = dot(jnp.concatenate([above, below], axis=0), high_t[...])
        rows = query.shape[0]
        conditioned = (stacked[:rows] + stacked[rows:] + dot(above, low_t[...])).astype(BF16)

        def block(g):
            start = pl.multiple_of(g * width, width)
            return dot(conditioned, train_t[:, pl.ds(start, width)])

        for other in range(n_x):
            part = block(2 * other + 1 - core).astype(BF16)
            for at, step in enumerate(steps):
                to_core[step, other] = part[at * count : (at + 1) * count]
        for step in steps:
            core_copy(step).start()
        for other in range(n_x):
            part = block(2 * other + core)
            for at, step in enumerate(steps):
                keep[step, other] = part[at * count : (at + 1) * count]

    def pair(step):
        core_copy(step).wait_recv()
        for hop in range(1, n_x):
            other = lax.rem(x + hop, n_x)
            to_chip[step, other] = (keep[step, other] + from_core[step, other].astype(F32)).astype(BF16)
            chip_copy(step, other).start()

    def finish(step):
        total = keep[step, x] + from_core[step, x].astype(F32)
        for hop in range(1, n_x):
            other = lax.rem(x + hop, n_x)
            chip_arrival(step, other).wait_recv()
            total += from_chip[step, other].astype(F32)
        rows = pl.ds(pl.multiple_of(shard_of(step) * count, count), count)
        scores_ref[rows, :] = total.astype(BF16)

    def turn(step, carry):
        @pl.when(jnp.logical_not(middle))
        def _():
            arrive(step)

        @pl.when(jnp.logical_and(middle, step < n_ex - 1))
        def _():
            arrive(step + 1)

        score((step,))
        pair(step)
        finish(step - 1)
        return carry

    score((0, 1))
    pair(0)
    pair(1)
    finish(0)
    lax.fori_loop(2, n_ex, turn, 0)
    finish(n_ex - 1)

    for part in range(PIECES):
        @pl.when(ex > 0)
        def _():
            passing(ex, part, 0, True).wait_send()

        @pl.when(ex < n_ex - 1)
        def _():
            passing(ex, part, 1, True).wait_send()

    def drain(step, carry):
        core_copy(step).wait_send()
        for hop in range(1, n_x):
            chip_copy(step, lax.rem(x + hop, n_x)).wait_send()

        @pl.when(step >= 1)
        def _():
            shard = shard_of(step)
            for part in range(PIECES):
                @pl.when(jnp.logical_and(shard > ex, ex > 0))
                def _():
                    passing(shard, part, 0).wait_send()

                @pl.when(jnp.logical_and(shard < ex, ex < n_ex - 1))
                def _():
                    passing(shard, part, 1).wait_send()

        return carry

    lax.fori_loop(0, n_ex, drain, 0)


def on_device(n_ex, n_lay, train_grads, queries, out_basis, in_basis, eigenvalues):
    n_x = n_lay // 2
    trains, flat = train_grads.shape[1:]
    count = queries.shape[1]
    width = trains // n_lay
    r_out, r_in = out_basis.shape[1], in_basis.shape[1]
    anywhere = pl.BlockSpec(memory_space=pl.ANY)
    dma = pltpu.SemaphoreType.DMA
    return pl.pallas_call(
        functools.partial(kernel, n_ex, n_x),
        out_shape=jax.ShapeDtypeStruct((n_ex * count, width), BF16),
        in_specs=[anywhere] * 5,
        out_specs=pl.BlockSpec(memory_space=pltpu.VMEM),
        scratch_shapes=[
            pltpu.VMEM((trains, flat), BF16),
            pltpu.VMEM((flat, trains), BF16),
            pltpu.VMEM((n_ex, count, flat), BF16),
            pltpu.VMEM((r_out, r_out), F32),
            pltpu.VMEM((r_in, r_in), F32),
            pltpu.VMEM((r_out, r_in), F32),
            pltpu.VMEM((r_out, flat), F32),
            pltpu.VMEM((flat, flat), BF16),
            pltpu.VMEM((flat, flat), BF16),
            pltpu.VMEM((flat, flat), BF16),
            pltpu.VMEM((flat, flat), BF16),
            pltpu.VMEM((1, flat), F32),
            pltpu.VMEM((n_ex, n_x, count, width), BF16),
            pltpu.VMEM((n_ex, n_x, count, width), BF16),
            pltpu.VMEM((n_ex, n_x, count, width), F32),
            pltpu.VMEM((n_ex, n_x, count, width), BF16),
            pltpu.VMEM((n_ex, n_x, count, width), BF16),
            dma((4,)),
            dma((n_lay,)),
            dma((2, n_ex, PIECES)),
            dma((n_ex, PIECES)),
            dma((n_ex,)),
            dma((n_ex,)),
            dma((n_ex, n_x)),
            dma((n_ex, n_x)),
        ],
        compiler_params=pltpu.CompilerParams(
            collective_id=0, has_side_effects=True, vmem_limit_bytes=56 * 1024 * 1024
        ),
        cost_estimate=pl.CostEstimate(
            flops=2 * n_ex * count * flat * (trains + 5 * flat),
            bytes_accessed=2 * (trains + count) * flat,
            transcendentals=0,
        ),
    )(train_grads, queries, out_basis, in_basis, eigenvalues)


def solution(mesh):
    placed = (
        P("lay", ("grp", "ex"), None),
        P("lay", ("grp", "ex"), None),
        P("lay", None, None),
        P("lay", None, None),
        P("lay", None, None),
    )
    return jax.shard_map(
        functools.partial(on_device, mesh.shape["ex"], mesh.shape["lay"]),
        mesh=mesh,
        in_specs=placed,
        out_specs=P("grp", ("ex", "lay")),
        check_vma=False,
    )
```

```python
import functools

import jax
import jax.numpy as jnp
from jax import lax
from jax.experimental import pallas as pl
from jax.experimental.pallas import tpu as pltpu
from jax.sharding import PartitionSpec as P

MESH = pl.DeviceIdType.MESH
F32 = jnp.float32
BF16 = jnp.bfloat16
PIECES = 2


def dot(a, b):
    return lax.dot_general(a, b, (((1,), (0,)), ((), ())), preferred_element_type=F32)


def dot_t(a, b):
    return lax.dot_general(a, b, (((1,), (1,)), ((), ())), preferred_element_type=F32)


def exact_dot(a, b):
    return jnp.dot(a, b, precision=lax.Precision.HIGHEST, preferred_element_type=F32)


def split(value):
    high = value.astype(BF16)
    return high, (value - high.astype(F32)).astype(BF16)


def kernel(
    n_ex, n_x,
    train_ref, query_ref, out_basis_ref, in_basis_ref, eigen_ref, scores_ref,
    train, held, out_mat, in_mat, eigen, wide_out, product, product_t, inverse,
    to_core, from_core, keep, to_chip, from_chip,
    local_sem, train_sem, gather_send, gather_recv, core_send, core_recv, chip_send, chip_recv,
):
    ex = lax.axis_index("ex")
    lay = lax.axis_index("lay")
    core = lax.rem(lay, 2)
    x = lax.div(lay, 2)
    n_lay = 2 * n_x
    width = train.shape[0] // n_lay
    count, flat = held.shape[1], held.shape[2]
    r_out, r_in = out_mat.shape[0], in_mat.shape[0]
    piece = count // PIECES
    middle = jnp.logical_and(ex > 0, ex < n_ex - 1)

    small = [
        pltpu.make_async_copy(out_basis_ref.at[0], out_mat, local_sem.at[0]),
        pltpu.make_async_copy(in_basis_ref.at[0], in_mat, local_sem.at[1]),
        pltpu.make_async_copy(eigen_ref.at[0], eigen, local_sem.at[2]),
        pltpu.make_async_copy(query_ref.at[0], held.at[ex], local_sem.at[3]),
    ]
    for copy in small:
        copy.start()

    barrier = pltpu.get_barrier_semaphore()

    @pl.when(ex > 0)
    def _():
        pl.semaphore_signal(barrier, inc=1, device_id={"ex": ex - 1}, device_id_type=MESH)

    @pl.when(ex < n_ex - 1)
    def _():
        pl.semaphore_signal(barrier, inc=1, device_id={"ex": ex + 1}, device_id_type=MESH)

    sibling = 2 * x + 1 - core
    pl.semaphore_signal(barrier, inc=1, device_id={"lay": sibling}, device_id_type=MESH)
    for step in range(1, n_x):
        other = lax.rem(x + step, n_x)
        pl.semaphore_signal(barrier, inc=1, device_id={"lay": 2 * other + core}, device_id_type=MESH)

    @pl.when(middle)
    def _():
        pl.semaphore_wait(barrier, n_x + 2)

    @pl.when(jnp.logical_not(middle))
    def _():
        pl.semaphore_wait(barrier, n_x + 1)

    def passing(shard, part, way, own=False):
        rows = pl.ds(part * piece, piece)
        return pltpu.make_async_remote_copy(
            src_ref=query_ref.at[0, rows] if own else held.at[shard, rows],
            dst_ref=held.at[shard, rows],
            send_sem=gather_send.at[way, shard, part],
            recv_sem=gather_recv.at[shard, part],
            device_id={"ex": ex + 2 * way - 1},
            device_id_type=MESH,
        )

    for part in range(PIECES):
        @pl.when(ex > 0)
        def _():
            passing(ex, part, 0, True).start()

        @pl.when(ex < n_ex - 1)
        def _():
            passing(ex, part, 1, True).start()

    blocks = [
        pltpu.make_async_copy(
            train_ref.at[0, pl.ds(g * width, width)], train.at[pl.ds(g * width, width)], train_sem.at[g]
        )
        for g in range(n_lay)
    ]
    for copy in blocks:
        copy.start()

    both = jnp.minimum(ex, n_ex - 1 - ex)

    def shard_of(step):
        near = lax.div(step + 1, 2)
        near_shard = jnp.where(lax.rem(step, 2) == 1, ex - near, ex + near)
        far = step - both
        far_shard = jnp.where(2 * ex < n_ex - 1, ex + far, ex - far)
        return jnp.where(step <= 2 * both, near_shard, far_shard)

    def arrive(step):
        shard = shard_of(step)
        for part in range(PIECES):
            passing(shard, part, 0).wait_recv()

            @pl.when(jnp.logical_and(shard > ex, ex > 0))
            def _():
                passing(shard, part, 0).start()

            @pl.when(jnp.logical_and(shard < ex, ex < n_ex - 1))
            def _():
                passing(shard, part, 1).start()

    for copy in small:
        copy.wait()
    column = lax.broadcasted_iota(jnp.int32, (r_in, flat), 1)
    inner = (lax.rem(column, r_in) == lax.broadcasted_iota(jnp.int32, (r_in, flat), 0)).astype(F32)
    outer_mask = lax.div(
        lax.broadcasted_iota(jnp.int32, (r_out, flat), 1), r_in
    ) == lax.broadcasted_iota(jnp.int32, (r_out, flat), 0)
    outer = outer_mask.astype(F32)
    wide_eigen = exact_dot(eigen[...], inner)
    damping = 0.1 * jnp.mean(eigen[...])
    line = jnp.sum(jnp.where(outer_mask, wide_eigen, 0.0), axis=0, keepdims=True)
    inverse[...] = 1.0 / (line + damping)

    def spread(out_part, in_part, target):
        wide_out[...] = exact_dot(out_part, outer)
        wide_in = exact_dot(in_part, inner)
        for a in range(r_out):
            target[a * r_in : (a + 1) * r_in, :] = (wide_in * wide_out[a : a + 1, :]).astype(BF16)

    spread(out_mat[...], in_mat[...], product)
    spread(out_mat[...].T, in_mat[...].T, product_t)

    @pl.when(middle)
    def _():
        arrive(1)
        arrive(2)

    for copy in blocks:
        copy.wait()

    @pl.when(jnp.logical_not(middle))
    def _():
        arrive(1)

    def core_copy(step):
        return pltpu.make_async_remote_copy(
            src_ref=to_core.at[step],
            dst_ref=from_core.at[step],
            send_sem=core_send.at[step],
            recv_sem=core_recv.at[step],
            device_id={"lay": sibling},
            device_id_type=MESH,
        )

    def chip_copy(step, other):
        return pltpu.make_async_remote_copy(
            src_ref=to_chip.at[step, other],
            dst_ref=from_chip.at[step, x],
            send_sem=chip_send.at[step, other],
            recv_sem=chip_recv.at[step, x],
            device_id={"lay": 2 * other + core},
            device_id_type=MESH,
        )

    def chip_arrival(step, other):
        return pltpu.make_async_remote_copy(
            src_ref=to_chip.at[step, other],
            dst_ref=from_chip.at[step, other],
            send_sem=chip_send.at[step, other],
            recv_sem=chip_recv.at[step, other],
            device_id={"lay": 2 * other + core},
            device_id_type=MESH,
        )

    def score(steps):
        query = jnp.concatenate([held[shard_of(step)] for step in steps], axis=0)
        rotated = dot(query, product[...])
        above, below = split(rotated * inverse[...])
        stacked = dot(jnp.concatenate([above, below], axis=0), product_t[...])
        rows = query.shape[0]
        conditioned = (stacked[:rows] + stacked[rows:]).astype(BF16)

        def block(g):
            start = pl.multiple_of(g * width, width)
            return dot_t(conditioned, train[pl.ds(start, width), :])

        for other in range(n_x):
            part = block(2 * other + 1 - core).astype(BF16)
            for at, step in enumerate(steps):
                to_core[step, other] = part[at * count : (at + 1) * count]
        for step in steps:
            core_copy(step).start()
        for other in range(n_x):
            part = block(2 * other + core)
            for at, step in enumerate(steps):
                keep[step, other] = part[at * count : (at + 1) * count]

    def pair(step):
        core_copy(step).wait_recv()
        for hop in range(1, n_x):
            other = lax.rem(x + hop, n_x)
            to_chip[step, other] = (keep[step, other] + from_core[step, other].astype(F32)).astype(BF16)
            chip_copy(step, other).start()

    def finish(step):
        total = keep[step, x] + from_core[step, x].astype(F32)
        for hop in range(1, n_x):
            other = lax.rem(x + hop, n_x)
            chip_arrival(step, other).wait_recv()
            total += from_chip[step, other].astype(F32)
        rows = pl.ds(pl.multiple_of(shard_of(step) * count, count), count)
        scores_ref[rows, :] = total.astype(BF16)

    def turn(step, carry):
        @pl.when(jnp.logical_not(middle))
        def _():
            arrive(step)

        @pl.when(jnp.logical_and(middle, step < n_ex - 1))
        def _():
            arrive(step + 1)

        score((step,))
        pair(step)
        finish(step - 1)
        return carry

    score((0, 1))
    pair(0)
    pair(1)
    finish(0)
    lax.fori_loop(2, n_ex, turn, 0)
    finish(n_ex - 1)

    for part in range(PIECES):
        @pl.when(ex > 0)
        def _():
            passing(ex, part, 0, True).wait_send()

        @pl.when(ex < n_ex - 1)
        def _():
            passing(ex, part, 1, True).wait_send()

    def drain(step, carry):
        core_copy(step).wait_send()
        for hop in range(1, n_x):
            chip_copy(step, lax.rem(x + hop, n_x)).wait_send()

        @pl.when(step >= 1)
        def _():
            shard = shard_of(step)
            for part in range(PIECES):
                @pl.when(jnp.logical_and(shard > ex, ex > 0))
                def _():
                    passing(shard, part, 0).wait_send()

                @pl.when(jnp.logical_and(shard < ex, ex < n_ex - 1))
                def _():
                    passing(shard, part, 1).wait_send()

        return carry

    lax.fori_loop(0, n_ex, drain, 0)


def on_device(n_ex, n_lay, train_grads, queries, out_basis, in_basis, eigenvalues):
    n_x = n_lay // 2
    trains, flat = train_grads.shape[1:]
    count = queries.shape[1]
    width = trains // n_lay
    r_out, r_in = out_basis.shape[1], in_basis.shape[1]
    anywhere = pl.BlockSpec(memory_space=pl.ANY)
    dma = pltpu.SemaphoreType.DMA
    return pl.pallas_call(
        functools.partial(kernel, n_ex, n_x),
        out_shape=jax.ShapeDtypeStruct((n_ex * count, width), BF16),
        in_specs=[anywhere] * 5,
        out_specs=pl.BlockSpec(memory_space=pltpu.VMEM),
        scratch_shapes=[
            pltpu.VMEM((trains, flat), BF16),
            pltpu.VMEM((n_ex, count, flat), BF16),
            pltpu.VMEM((r_out, r_out), F32),
            pltpu.VMEM((r_in, r_in), F32),
            pltpu.VMEM((r_out, r_in), F32),
            pltpu.VMEM((r_out, flat), F32),
            pltpu.VMEM((flat, flat), BF16),
            pltpu.VMEM((flat, flat), BF16),
            pltpu.VMEM((1, flat), F32),
            pltpu.VMEM((n_ex, n_x, count, width), BF16),
            pltpu.VMEM((n_ex, n_x, count, width), BF16),
            pltpu.VMEM((n_ex, n_x, count, width), F32),
            pltpu.VMEM((n_ex, n_x, count, width), BF16),
            pltpu.VMEM((n_ex, n_x, count, width), BF16),
            dma((4,)),
            dma((n_lay,)),
            dma((2, n_ex, PIECES)),
            dma((n_ex, PIECES)),
            dma((n_ex,)),
            dma((n_ex,)),
            dma((n_ex, n_x)),
            dma((n_ex, n_x)),
        ],
        compiler_params=pltpu.CompilerParams(
            collective_id=0, has_side_effects=True, vmem_limit_bytes=56 * 1024 * 1024
        ),
        cost_estimate=pl.CostEstimate(
            flops=2 * n_ex * count * flat * (trains + 3 * flat),
            bytes_accessed=2 * (trains + count) * flat,
            transcendentals=0,
        ),
    )(train_grads, queries, out_basis, in_basis, eigenvalues)


def solution(mesh):
    placed = (
        P("lay", ("grp", "ex"), None),
        P("lay", ("grp", "ex"), None),
        P("lay", None, None),
        P("lay", None, None),
        P("lay", None, None),
    )
    return jax.shard_map(
        functools.partial(on_device, mesh.shape["ex"], mesh.shape["lay"]),
        mesh=mesh,
        in_specs=placed,
        out_specs=P("grp", ("ex", "lay")),
        check_vma=False,
    )
```

```python
import functools

import jax
import jax.numpy as jnp
from jax import lax
from jax.experimental import pallas as pl
from jax.experimental.pallas import tpu as pltpu
from jax.sharding import PartitionSpec as P

MESH = pl.DeviceIdType.MESH
F32 = jnp.float32
BF16 = jnp.bfloat16
PIECES = 2


def dot(a, b):
    return lax.dot_general(a, b, (((1,), (0,)), ((), ())), preferred_element_type=F32)


def dot_t(a, b):
    return lax.dot_general(a, b, (((1,), (1,)), ((), ())), preferred_element_type=F32)


def exact_dot(a, b):
    return jnp.dot(a, b, precision=lax.Precision.HIGHEST, preferred_element_type=F32)


def split(value):
    high = value.astype(BF16)
    return high, (value - high.astype(F32)).astype(BF16)


def kernel(
    n_ex, n_x,
    train_ref, query_ref, out_basis_ref, in_basis_ref, eigen_ref, scores_ref,
    train, held, out_mat, in_mat, eigen, wide_out, product, product_t, inverse,
    to_core, from_core, keep, to_chip, from_chip,
    local_sem, train_sem, gather_send, gather_recv, core_send, core_recv, chip_send, chip_recv,
):
    ex = lax.axis_index("ex")
    lay = lax.axis_index("lay")
    core = lax.rem(lay, 2)
    x = lax.div(lay, 2)
    n_lay = 2 * n_x
    width = train.shape[0] // n_lay
    count, flat = held.shape[1], held.shape[2]
    r_out, r_in = out_mat.shape[0], in_mat.shape[0]
    piece = count // PIECES
    middle = jnp.logical_and(ex > 0, ex < n_ex - 1)

    small = [
        pltpu.make_async_copy(out_basis_ref.at[0], out_mat, local_sem.at[0]),
        pltpu.make_async_copy(in_basis_ref.at[0], in_mat, local_sem.at[1]),
        pltpu.make_async_copy(eigen_ref.at[0], eigen, local_sem.at[2]),
        pltpu.make_async_copy(query_ref.at[0], held.at[ex], local_sem.at[3]),
    ]
    for copy in small:
        copy.start()

    barrier = pltpu.get_barrier_semaphore()

    @pl.when(ex > 0)
    def _():
        pl.semaphore_signal(barrier, inc=1, device_id={"ex": ex - 1}, device_id_type=MESH)

    @pl.when(ex < n_ex - 1)
    def _():
        pl.semaphore_signal(barrier, inc=1, device_id={"ex": ex + 1}, device_id_type=MESH)

    sibling = 2 * x + 1 - core
    pl.semaphore_signal(barrier, inc=1, device_id={"lay": sibling}, device_id_type=MESH)
    for step in range(1, n_x):
        other = lax.rem(x + step, n_x)
        pl.semaphore_signal(barrier, inc=1, device_id={"lay": 2 * other + core}, device_id_type=MESH)

    @pl.when(middle)
    def _():
        pl.semaphore_wait(barrier, n_x + 2)

    @pl.when(jnp.logical_not(middle))
    def _():
        pl.semaphore_wait(barrier, n_x + 1)

    def passing(shard, part, way, own=False):
        rows = pl.ds(part * piece, piece)
        return pltpu.make_async_remote_copy(
            src_ref=query_ref.at[0, rows] if own else held.at[shard, rows],
            dst_ref=held.at[shard, rows],
            send_sem=gather_send.at[way, shard, part],
            recv_sem=gather_recv.at[shard, part],
            device_id={"ex": ex + 2 * way - 1},
            device_id_type=MESH,
        )

    for part in range(PIECES):
        @pl.when(ex > 0)
        def _():
            passing(ex, part, 0, True).start()

        @pl.when(ex < n_ex - 1)
        def _():
            passing(ex, part, 1, True).start()

    blocks = [
        pltpu.make_async_copy(
            train_ref.at[0, pl.ds(g * width, width)], train.at[pl.ds(g * width, width)], train_sem.at[g]
        )
        for g in range(n_lay)
    ]
    for copy in blocks:
        copy.start()

    both = jnp.minimum(ex, n_ex - 1 - ex)

    def shard_of(step):
        near = lax.div(step + 1, 2)
        near_shard = jnp.where(lax.rem(step, 2) == 1, ex - near, ex + near)
        far = step - both
        far_shard = jnp.where(2 * ex < n_ex - 1, ex + far, ex - far)
        return jnp.where(step <= 2 * both, near_shard, far_shard)

    def arrive(step):
        shard = shard_of(step)
        for part in range(PIECES):
            passing(shard, part, 0).wait_recv()

            @pl.when(jnp.logical_and(shard > ex, ex > 0))
            def _():
                passing(shard, part, 0).start()

            @pl.when(jnp.logical_and(shard < ex, ex < n_ex - 1))
            def _():
                passing(shard, part, 1).start()

    for copy in small:
        copy.wait()
    column = lax.broadcasted_iota(jnp.int32, (r_in, flat), 1)
    inner = (lax.rem(column, r_in) == lax.broadcasted_iota(jnp.int32, (r_in, flat), 0)).astype(F32)
    outer_mask = lax.div(
        lax.broadcasted_iota(jnp.int32, (r_out, flat), 1), r_in
    ) == lax.broadcasted_iota(jnp.int32, (r_out, flat), 0)
    outer = outer_mask.astype(F32)
    wide_eigen = exact_dot(eigen[...], inner)
    damping = 0.1 * jnp.mean(eigen[...])
    line = jnp.sum(jnp.where(outer_mask, wide_eigen, 0.0), axis=0, keepdims=True)
    inverse[...] = 1.0 / (line + damping)

    def spread(out_part, in_part, target):
        wide_out[...] = exact_dot(out_part, outer)
        wide_in = exact_dot(in_part, inner)
        for a in range(r_out):
            target[a * r_in : (a + 1) * r_in, :] = (wide_in * wide_out[a : a + 1, :]).astype(BF16)

    spread(out_mat[...], in_mat[...], product)
    spread(out_mat[...].T, in_mat[...].T, product_t)

    @pl.when(middle)
    def _():
        arrive(1)
        arrive(2)

    for copy in blocks:
        copy.wait()

    @pl.when(jnp.logical_not(middle))
    def _():
        arrive(1)

    def core_copy(step, other):
        return pltpu.make_async_remote_copy(
            src_ref=to_core.at[step, other],
            dst_ref=from_core.at[step, other],
            send_sem=core_send.at[step, other],
            recv_sem=core_recv.at[step, other],
            device_id={"lay": sibling},
            device_id_type=MESH,
        )

    def chip_copy(step, other):
        return pltpu.make_async_remote_copy(
            src_ref=to_chip.at[step, other],
            dst_ref=from_chip.at[step, x],
            send_sem=chip_send.at[step, other],
            recv_sem=chip_recv.at[step, x],
            device_id={"lay": 2 * other + core},
            device_id_type=MESH,
        )

    def chip_arrival(step, other):
        return pltpu.make_async_remote_copy(
            src_ref=to_chip.at[step, other],
            dst_ref=from_chip.at[step, other],
            send_sem=chip_send.at[step, other],
            recv_sem=chip_recv.at[step, other],
            device_id={"lay": 2 * other + core},
            device_id_type=MESH,
        )

    def score(steps):
        query = jnp.concatenate([held[shard_of(step)] for step in steps], axis=0)
        rotated = dot(query, product[...])
        above, below = split(rotated * inverse[...])
        stacked = dot(jnp.concatenate([above, below], axis=0), product_t[...])
        rows = query.shape[0]
        conditioned = (stacked[:rows] + stacked[rows:]).astype(BF16)

        def block(g):
            start = pl.multiple_of(g * width, width)
            return dot_t(conditioned, train[pl.ds(start, width), :])

        def give(other):
            part = block(2 * other + 1 - core).astype(BF16)
            for at, step in enumerate(steps):
                to_core[step, other] = part[at * count : (at + 1) * count]
            for step in steps:
                core_copy(step, other).start()

        def hold(other):
            part = block(2 * other + core)
            for at, step in enumerate(steps):
                keep[step, other] = part[at * count : (at + 1) * count]

        for hop in range(1, n_x):
            give(lax.rem(x + hop, n_x))
        for hop in range(1, n_x):
            hold(lax.rem(x + hop, n_x))
        give(x)
        for step in steps:
            pair(step)
        hold(x)

    def pair(step):
        for hop in range(1, n_x):
            other = lax.rem(x + hop, n_x)
            core_copy(step, other).wait_recv()
            to_chip[step, other] = (keep[step, other] + from_core[step, other].astype(F32)).astype(BF16)
            chip_copy(step, other).start()

    def finish(step):
        core_copy(step, x).wait_recv()
        total = keep[step, x] + from_core[step, x].astype(F32)
        for hop in range(1, n_x):
            other = lax.rem(x + hop, n_x)
            chip_arrival(step, other).wait_recv()
            total += from_chip[step, other].astype(F32)
        rows = pl.ds(pl.multiple_of(shard_of(step) * count, count), count)
        scores_ref[rows, :] = total.astype(BF16)

    def turn(step, carry):
        @pl.when(jnp.logical_not(middle))
        def _():
            arrive(step)

        @pl.when(jnp.logical_and(middle, step < n_ex - 1))
        def _():
            arrive(step + 1)

        score((step,))
        finish(step - 1)
        return carry

    score((0, 1))
    finish(0)
    lax.fori_loop(2, n_ex, turn, 0)
    finish(n_ex - 1)

    for part in range(PIECES):
        @pl.when(ex > 0)
        def _():
            passing(ex, part, 0, True).wait_send()

        @pl.when(ex < n_ex - 1)
        def _():
            passing(ex, part, 1, True).wait_send()

    def drain(step, carry):
        core_copy(step, x).wait_send()
        for hop in range(1, n_x):
            other = lax.rem(x + hop, n_x)
            core_copy(step, other).wait_send()
            chip_copy(step, other).wait_send()

        @pl.when(step >= 1)
        def _():
            shard = shard_of(step)
            for part in range(PIECES):
                @pl.when(jnp.logical_and(shard > ex, ex > 0))
                def _():
                    passing(shard, part, 0).wait_send()

                @pl.when(jnp.logical_and(shard < ex, ex < n_ex - 1))
                def _():
                    passing(shard, part, 1).wait_send()

        return carry

    lax.fori_loop(0, n_ex, drain, 0)


def on_device(n_ex, n_lay, train_grads, queries, out_basis, in_basis, eigenvalues):
    n_x = n_lay // 2
    trains, flat = train_grads.shape[1:]
    count = queries.shape[1]
    width = trains // n_lay
    r_out, r_in = out_basis.shape[1], in_basis.shape[1]
    anywhere = pl.BlockSpec(memory_space=pl.ANY)
    dma = pltpu.SemaphoreType.DMA
    return pl.pallas_call(
        functools.partial(kernel, n_ex, n_x),
        out_shape=jax.ShapeDtypeStruct((n_ex * count, width), BF16),
        in_specs=[anywhere] * 5,
        out_specs=pl.BlockSpec(memory_space=pltpu.VMEM),
        scratch_shapes=[
            pltpu.VMEM((trains, flat), BF16),
            pltpu.VMEM((n_ex, count, flat), BF16),
            pltpu.VMEM((r_out, r_out), F32),
            pltpu.VMEM((r_in, r_in), F32),
            pltpu.VMEM((r_out, r_in), F32),
            pltpu.VMEM((r_out, flat), F32),
            pltpu.VMEM((flat, flat), BF16),
            pltpu.VMEM((flat, flat), BF16),
            pltpu.VMEM((1, flat), F32),
            pltpu.VMEM((n_ex, n_x, count, width), BF16),
            pltpu.VMEM((n_ex, n_x, count, width), BF16),
            pltpu.VMEM((n_ex, n_x, count, width), F32),
            pltpu.VMEM((n_ex, n_x, count, width), BF16),
            pltpu.VMEM((n_ex, n_x, count, width), BF16),
            dma((4,)),
            dma((n_lay,)),
            dma((2, n_ex, PIECES)),
            dma((n_ex, PIECES)),
            dma((n_ex, n_x)),
            dma((n_ex, n_x)),
            dma((n_ex, n_x)),
            dma((n_ex, n_x)),
        ],
        compiler_params=pltpu.CompilerParams(
            collective_id=0, has_side_effects=True, vmem_limit_bytes=56 * 1024 * 1024
        ),
        cost_estimate=pl.CostEstimate(
            flops=2 * n_ex * count * flat * (trains + 3 * flat),
            bytes_accessed=2 * (trains + count) * flat,
            transcendentals=0,
        ),
    )(train_grads, queries, out_basis, in_basis, eigenvalues)


def solution(mesh):
    placed = (
        P("lay", ("grp", "ex"), None),
        P("lay", ("grp", "ex"), None),
        P("lay", None, None),
        P("lay", None, None),
        P("lay", None, None),
    )
    return jax.shard_map(
        functools.partial(on_device, mesh.shape["ex"], mesh.shape["lay"]),
        mesh=mesh,
        in_specs=placed,
        out_specs=P("grp", ("ex", "lay")),
        check_vma=False,
    )
```

```python
import functools

import jax
import jax.numpy as jnp
from jax import lax
from jax.experimental import pallas as pl
from jax.experimental.pallas import tpu as pltpu
from jax.sharding import PartitionSpec as P

MESH = pl.DeviceIdType.MESH
F32 = jnp.float32
BF16 = jnp.bfloat16
PIECES = 2


def dot(a, b):
    return lax.dot_general(a, b, (((1,), (0,)), ((), ())), preferred_element_type=F32)


def dot_t(a, b):
    return lax.dot_general(a, b, (((1,), (1,)), ((), ())), preferred_element_type=F32)


def exact_dot(a, b):
    return jnp.dot(a, b, precision=lax.Precision.HIGHEST, preferred_element_type=F32)


def split(value):
    high = value.astype(BF16)
    return high, (value - high.astype(F32)).astype(BF16)


def kernel(
    n_ex, n_x,
    train_ref, query_ref, out_basis_ref, in_basis_ref, eigen_ref, scores_ref,
    train, held, out_mat, in_mat, eigen, wide_out, product, product_t, inverse,
    to_core, from_core, keep, to_chip, from_chip, result, result_sem,
    local_sem, train_sem, gather_send, gather_recv, core_send, core_recv, chip_send, chip_recv,
):
    ex = lax.axis_index("ex")
    lay = lax.axis_index("lay")
    core = lax.rem(lay, 2)
    x = lax.div(lay, 2)
    n_lay = 2 * n_x
    width = train.shape[0] // n_lay
    count, flat = held.shape[1], held.shape[2]
    r_out, r_in = out_mat.shape[0], in_mat.shape[0]
    piece = count // PIECES
    middle = jnp.logical_and(ex > 0, ex < n_ex - 1)

    small = [
        pltpu.make_async_copy(out_basis_ref.at[0], out_mat, local_sem.at[0]),
        pltpu.make_async_copy(in_basis_ref.at[0], in_mat, local_sem.at[1]),
        pltpu.make_async_copy(eigen_ref.at[0], eigen, local_sem.at[2]),
        pltpu.make_async_copy(query_ref.at[0], held.at[ex], local_sem.at[3]),
    ]
    for copy in small:
        copy.start()

    barrier = pltpu.get_barrier_semaphore()

    @pl.when(ex > 0)
    def _():
        pl.semaphore_signal(barrier, inc=1, device_id={"ex": ex - 1}, device_id_type=MESH)

    @pl.when(ex < n_ex - 1)
    def _():
        pl.semaphore_signal(barrier, inc=1, device_id={"ex": ex + 1}, device_id_type=MESH)

    sibling = 2 * x + 1 - core
    pl.semaphore_signal(barrier, inc=1, device_id={"lay": sibling}, device_id_type=MESH)
    for step in range(1, n_x):
        other = lax.rem(x + step, n_x)
        pl.semaphore_signal(barrier, inc=1, device_id={"lay": 2 * other + core}, device_id_type=MESH)

    @pl.when(middle)
    def _():
        pl.semaphore_wait(barrier, n_x + 2)

    @pl.when(jnp.logical_not(middle))
    def _():
        pl.semaphore_wait(barrier, n_x + 1)

    def passing(shard, part, way, own=False):
        rows = pl.ds(part * piece, piece)
        return pltpu.make_async_remote_copy(
            src_ref=query_ref.at[0, rows] if own else held.at[shard, rows],
            dst_ref=held.at[shard, rows],
            send_sem=gather_send.at[way, shard, part],
            recv_sem=gather_recv.at[shard, part],
            device_id={"ex": ex + 2 * way - 1},
            device_id_type=MESH,
        )

    for part in range(PIECES):
        @pl.when(ex > 0)
        def _():
            passing(ex, part, 0, True).start()

        @pl.when(ex < n_ex - 1)
        def _():
            passing(ex, part, 1, True).start()

    blocks = [
        pltpu.make_async_copy(
            train_ref.at[0, pl.ds(g * width, width)], train.at[pl.ds(g * width, width)], train_sem.at[g]
        )
        for g in range(n_lay)
    ]
    for copy in blocks:
        copy.start()

    both = jnp.minimum(ex, n_ex - 1 - ex)

    def shard_of(step):
        near = lax.div(step + 1, 2)
        near_shard = jnp.where(lax.rem(step, 2) == 1, ex - near, ex + near)
        far = step - both
        far_shard = jnp.where(2 * ex < n_ex - 1, ex + far, ex - far)
        return jnp.where(step <= 2 * both, near_shard, far_shard)

    def arrive(step):
        shard = shard_of(step)
        for part in range(PIECES):
            passing(shard, part, 0).wait_recv()

            @pl.when(jnp.logical_and(shard > ex, ex > 0))
            def _():
                passing(shard, part, 0).start()

            @pl.when(jnp.logical_and(shard < ex, ex < n_ex - 1))
            def _():
                passing(shard, part, 1).start()

    for copy in small:
        copy.wait()
    column = lax.broadcasted_iota(jnp.int32, (r_in, flat), 1)
    inner = (lax.rem(column, r_in) == lax.broadcasted_iota(jnp.int32, (r_in, flat), 0)).astype(F32)
    outer_mask = lax.div(
        lax.broadcasted_iota(jnp.int32, (r_out, flat), 1), r_in
    ) == lax.broadcasted_iota(jnp.int32, (r_out, flat), 0)
    outer = outer_mask.astype(F32)
    wide_eigen = exact_dot(eigen[...], inner)
    damping = 0.1 * jnp.mean(eigen[...])
    line = jnp.sum(jnp.where(outer_mask, wide_eigen, 0.0), axis=0, keepdims=True)
    inverse[...] = 1.0 / (line + damping)

    def spread(out_part, in_part, target):
        wide_out[...] = exact_dot(out_part, outer)
        wide_in = exact_dot(in_part, inner)
        for a in range(r_out):
            target[a * r_in : (a + 1) * r_in, :] = (wide_in * wide_out[a : a + 1, :]).astype(BF16)

    spread(out_mat[...], in_mat[...], product)
    spread(out_mat[...].T, in_mat[...].T, product_t)

    @pl.when(middle)
    def _():
        arrive(1)
        arrive(2)

    for copy in blocks:
        copy.wait()

    @pl.when(jnp.logical_not(middle))
    def _():
        arrive(1)

    def core_copy(step, other):
        return pltpu.make_async_remote_copy(
            src_ref=to_core.at[step, other],
            dst_ref=from_core.at[step, other],
            send_sem=core_send.at[step, other],
            recv_sem=core_recv.at[step, other],
            device_id={"lay": sibling},
            device_id_type=MESH,
        )

    def chip_copy(step, other):
        return pltpu.make_async_remote_copy(
            src_ref=to_chip.at[step, other],
            dst_ref=from_chip.at[step, x],
            send_sem=chip_send.at[step, other],
            recv_sem=chip_recv.at[step, x],
            device_id={"lay": 2 * other + core},
            device_id_type=MESH,
        )

    def chip_arrival(step, other):
        return pltpu.make_async_remote_copy(
            src_ref=to_chip.at[step, other],
            dst_ref=from_chip.at[step, other],
            send_sem=chip_send.at[step, other],
            recv_sem=chip_recv.at[step, other],
            device_id={"lay": 2 * other + core},
            device_id_type=MESH,
        )

    def score(steps):
        query = jnp.concatenate([held[shard_of(step)] for step in steps], axis=0)
        rotated = dot(query, product[...])
        above, below = split(rotated * inverse[...])
        stacked = dot(jnp.concatenate([above, below], axis=0), product_t[...])
        rows = query.shape[0]
        conditioned = (stacked[:rows] + stacked[rows:]).astype(BF16)

        def block(g):
            start = pl.multiple_of(g * width, width)
            return dot_t(conditioned, train[pl.ds(start, width), :])

        def give(other):
            part = block(2 * other + 1 - core).astype(BF16)
            for at, step in enumerate(steps):
                to_core[step, other] = part[at * count : (at + 1) * count]
            for step in steps:
                core_copy(step, other).start()

        def hold(other):
            part = block(2 * other + core)
            for at, step in enumerate(steps):
                keep[step, other] = part[at * count : (at + 1) * count]

        for hop in range(1, n_x):
            give(lax.rem(x + hop, n_x))
        for hop in range(1, n_x):
            hold(lax.rem(x + hop, n_x))
        give(x)
        for step in steps:
            pair(step)
        hold(x)

    def pair(step):
        for hop in range(1, n_x):
            other = lax.rem(x + hop, n_x)
            core_copy(step, other).wait_recv()
            to_chip[step, other] = (keep[step, other] + from_core[step, other].astype(F32)).astype(BF16)
            chip_copy(step, other).start()

    def result_copy(step):
        rows = pl.ds(pl.multiple_of(shard_of(step) * count, count), count)
        return pltpu.make_async_copy(result.at[rows], scores_ref.at[rows], result_sem.at[step])

    def finish(step):
        core_copy(step, x).wait_recv()
        total = keep[step, x] + from_core[step, x].astype(F32)
        for hop in range(1, n_x):
            other = lax.rem(x + hop, n_x)
            chip_arrival(step, other).wait_recv()
            total += from_chip[step, other].astype(F32)
        rows = pl.ds(pl.multiple_of(shard_of(step) * count, count), count)
        result[rows, :] = total.astype(BF16)
        result_copy(step).start()

    def turn(step, carry):
        @pl.when(jnp.logical_not(middle))
        def _():
            arrive(step)

        @pl.when(jnp.logical_and(middle, step < n_ex - 1))
        def _():
            arrive(step + 1)

        score((step,))
        finish(step - 1)
        return carry

    score((0, 1))
    finish(0)
    lax.fori_loop(2, n_ex, turn, 0)
    finish(n_ex - 1)

    for part in range(PIECES):
        @pl.when(ex > 0)
        def _():
            passing(ex, part, 0, True).wait_send()

        @pl.when(ex < n_ex - 1)
        def _():
            passing(ex, part, 1, True).wait_send()

    def drain(step, carry):
        result_copy(step).wait()
        core_copy(step, x).wait_send()
        for hop in range(1, n_x):
            other = lax.rem(x + hop, n_x)
            core_copy(step, other).wait_send()
            chip_copy(step, other).wait_send()

        @pl.when(step >= 1)
        def _():
            shard = shard_of(step)
            for part in range(PIECES):
                @pl.when(jnp.logical_and(shard > ex, ex > 0))
                def _():
                    passing(shard, part, 0).wait_send()

                @pl.when(jnp.logical_and(shard < ex, ex < n_ex - 1))
                def _():
                    passing(shard, part, 1).wait_send()

        return carry

    lax.fori_loop(0, n_ex, drain, 0)


def on_device(n_ex, n_lay, train_grads, queries, out_basis, in_basis, eigenvalues):
    n_x = n_lay // 2
    trains, flat = train_grads.shape[1:]
    count = queries.shape[1]
    width = trains // n_lay
    r_out, r_in = out_basis.shape[1], in_basis.shape[1]
    anywhere = pl.BlockSpec(memory_space=pl.ANY)
    dma = pltpu.SemaphoreType.DMA
    return pl.pallas_call(
        functools.partial(kernel, n_ex, n_x),
        out_shape=jax.ShapeDtypeStruct((n_ex * count, width), BF16),
        in_specs=[anywhere] * 5,
        out_specs=anywhere,
        scratch_shapes=[
            pltpu.VMEM((trains, flat), BF16),
            pltpu.VMEM((n_ex, count, flat), BF16),
            pltpu.VMEM((r_out, r_out), F32),
            pltpu.VMEM((r_in, r_in), F32),
            pltpu.VMEM((r_out, r_in), F32),
            pltpu.VMEM((r_out, flat), F32),
            pltpu.VMEM((flat, flat), BF16),
            pltpu.VMEM((flat, flat), BF16),
            pltpu.VMEM((1, flat), F32),
            pltpu.VMEM((n_ex, n_x, count, width), BF16),
            pltpu.VMEM((n_ex, n_x, count, width), BF16),
            pltpu.VMEM((n_ex, n_x, count, width), F32),
            pltpu.VMEM((n_ex, n_x, count, width), BF16),
            pltpu.VMEM((n_ex, n_x, count, width), BF16),
            pltpu.VMEM((n_ex * count, width), BF16),
            dma((n_ex,)),
            dma((4,)),
            dma((n_lay,)),
            dma((2, n_ex, PIECES)),
            dma((n_ex, PIECES)),
            dma((n_ex, n_x)),
            dma((n_ex, n_x)),
            dma((n_ex, n_x)),
            dma((n_ex, n_x)),
        ],
        compiler_params=pltpu.CompilerParams(
            collective_id=0, has_side_effects=True, vmem_limit_bytes=56 * 1024 * 1024
        ),
        cost_estimate=pl.CostEstimate(
            flops=2 * n_ex * count * flat * (trains + 3 * flat),
            bytes_accessed=2 * (trains + count) * flat,
            transcendentals=0,
        ),
    )(train_grads, queries, out_basis, in_basis, eigenvalues)


def solution(mesh):
    placed = (
        P("lay", ("grp", "ex"), None),
        P("lay", ("grp", "ex"), None),
        P("lay", None, None),
        P("lay", None, None),
        P("lay", None, None),
    )
    return jax.shard_map(
        functools.partial(on_device, mesh.shape["ex"], mesh.shape["lay"]),
        mesh=mesh,
        in_specs=placed,
        out_specs=P("grp", ("ex", "lay")),
        check_vma=False,
    )
```
